32 devices in a mesh: dp: 8 (over z, y), tensor: 4 (over x, core).
Axes of the slice: x: 2, y: 2, z: 4, core: 2. Of those that a mesh axis runs over, the one named last changes fastest.
Arguments:
- normed_input: bfloat16 [8192, 8192], P(('dp', 'tensor')), may hold values from -6 to 6
- grad_kv: bfloat16 [2048, 2048], P('dp', 'tensor'), may hold values from -6 to 6
- kept: int32 [8, 256], P('dp'), may hold values from 0 to 1023, as said below
Outputs:
- weight_grad: float32 [8192, 2048], P('dp', 'tensor')
The draws below stay inside these ranges and needn't reach their ends.
Inputs may be any that keep to these rules, and one draw needn't show every extreme that they name: `kept`: row g lists 256 distinct row numbers of data group g in rising order. Among the 256 rows of any one device of the group at most 128 are listed, and in every group some device has exactly 128 listed.
All inputs are finite; a program needn't handle non-finite values.
Results may differ from the reference program's by a relative error of at most 0.0003.
Values may be sent and summed in bfloat16 or wider, within the bound.
A program may use at most 128 MiB of HBM per device.

```python
import jax
import jax.numpy as jnp
from jax import lax

D = 8192
TOK_DEV = 256
KV_COLS = 2048
GROUP = 1024
KEEP = 256
CAP = 128
TOKENS = 8192
N_DP = 8
N_TENSOR = 4


def kept_group(key):
    heavy = jax.random.randint(jax.random.fold_in(key, 1), (), 0, N_TENSOR)
    remaining = jnp.array(KEEP - CAP, jnp.int32)
    counts = [jnp.array(CAP, jnp.int32)]
    for shard in range(N_TENSOR - 2):
        later = N_TENSOR - 2 - shard
        lowest = jnp.maximum(0, remaining - CAP * later)
        highest = jnp.minimum(CAP, remaining)
        picked = jax.random.randint(jax.random.fold_in(key, 10 + shard), (), lowest, highest + 1).astype(jnp.int32)
        counts.append(picked)
        remaining = remaining - picked
    counts.append(remaining)
    shard_counts = jnp.roll(jnp.stack(counts), heavy)
    shard_keys = jax.random.split(jax.random.fold_in(key, 2), N_TENSOR)
    ranks = jax.vmap(lambda one: jax.random.permutation(one, TOK_DEV))(shard_keys)
    chosen = (ranks < shard_counts[:, None]).reshape(GROUP)
    places = jnp.arange(GROUP, dtype=jnp.int32)
    order = jnp.argsort(jnp.where(chosen, places, GROUP + places))
    return order[:KEEP].astype(jnp.int32)


def draw_kept(key, part):
    key = jax.random.fold_in(key, 7)
    group_keys = jax.random.split(key, N_DP)
    return jax.vmap(kept_group)(group_keys)


def strengthened(entries, rng, source, target, shards_of, factor):
    owner, partner = [(jnp.arange(entries.shape[axis_at]) // (entries.shape[axis_at] // shards_of)).reshape([-1 if axis == axis_at else 1 for axis in range(entries.ndim)]) for axis_at in (source, target)]
    chosen = jax.random.permutation(rng, shards_of)[partner]
    strong = (owner == chosen) | (owner == (partner + shards_of // 2) % shards_of)
    return jnp.where(strong, factor * entries, entries)


def level_of(own_key, dims, cuts, least, high):
    def one(axis_at, shards_of):
        steps = jax.random.uniform(jax.random.fold_in(jax.random.fold_in(own_key, 6), axis_at), (shards_of,), jnp.float32, least / len(cuts), high / len(cuts))
        return jnp.repeat(jnp.exp(steps), dims[axis_at] // shards_of).reshape((-1,) + (1,) * (len(dims) - axis_at - 1))

    factor_of = one(*cuts[0])
    for cut in cuts[1:]:
        factor_of = factor_of * one(*cut)
    return factor_of


def noise(own_key, extent, scale, bound, pieces=(), kind=jnp.bfloat16):
    loudness = level_of(own_key, extent, pieces, -0.22, 0.18) if pieces else 1.0
    entries = jax.random.normal(own_key, extent, jnp.float32) * scale * loudness
    return jnp.minimum(jnp.maximum(entries, -bound), bound).astype(kind)


def heavy_noise(rng, dims, width, reach, cuts, heavy, held_as=jnp.bfloat16):
    entries = width * jax.random.normal(rng, dims, jnp.float32)
    if cuts:
        entries = entries * level_of(rng, dims, cuts, -0.22, 0.18)
    return jnp.clip(strengthened(entries, jax.random.fold_in(rng, 3), *heavy), -reach, reach).astype(held_as)


def setup_inputs(seed: int = 0) -> dict:
    splits = jax.random.split(jax.random.key(seed), 4)
    return {
        "normed_input": heavy_noise(splits[0], (TOKENS, D), 1.0, 6.0, ((0, 32),), (0, 1, 32, 2.75)),
        "grad_kv": noise(splits[1], (N_DP * KEEP, KV_COLS), 1.0, 6.0, ((0, 8), (1, 4))),
        "kept": draw_kept(jax.random.fold_in(splits[3], 71), 0),
    }


def reference(normed_input, grad_kv, kept):
    groups = normed_input.reshape(N_DP, GROUP, D)
    grads = grad_kv.reshape(N_DP, KEEP, KV_COLS)

    def accumulate(total, item):
        rows, grad_rows, listed = item
        selected = rows[listed.astype(jnp.int32)]
        term = jnp.dot(selected.T, grad_rows, preferred_element_type=jnp.float32)
        return total + term, None

    total, _ = lax.scan(accumulate, jnp.zeros((D, KV_COLS), jnp.float32), (groups, grads, kept))
    return total * (GROUP / KEEP)
```

```python
import functools

import jax
import jax.numpy as jnp
from jax import lax
from jax.experimental import pallas as pl
from jax.experimental.pallas import tpu as pltpu
from jax.sharding import PartitionSpec as P

MESH = pl.DeviceIdType.MESH
CHUNK = 256


def flip(value, bits):
    place = 1
    result = value
    while place <= bits:
        if bits & place:
            result = result + place * (1 - 2 * ((value // place) % 2))
        place *= 2
    return result


def turn_of(rank):
    across, core = rank // 2, rank % 2
    return 2 * core + (across + core) % 2


def meet(group, turn, j):
    low = (group % 2 + turn % 2) % 2 + 2 * ((group // 2 % 2 + turn // 2) % 2)
    return low + 4 * flip(group // 4, j)


def kernel(
    n_dp, chunk, scale,
    x_hbm, grad_hbm, kept_ref, out_ref,
    x_buf, pick, pre, comp, sel, grads,
    x_sem, own_sem, pre_send, pre_recv, sel_send, sel_recv, grad_send, grad_recv,
):
    tok = x_hbm.shape[0]
    keep = kept_ref.shape[1]
    cap = tok // 2
    cols = x_hbm.shape[1] // n_dp
    halves = cols // chunk
    blocks = n_dp // 4
    me = lax.axis_index("dp")
    rank = lax.axis_index("tensor")
    turn = turn_of(rank)
    turns = [turn_of(flip(rank, r)) for r in range(4)]
    steps = [(j, h) for j in reversed(range(blocks)) for h in range(halves)]

    def x_copy(j, r):
        start = pl.multiple_of(meet(me, turns[r], j) * cols, cols)
        return pltpu.make_async_copy(
            x_hbm.at[:, pl.ds(start, cols)], x_buf.at[j, r], x_sem.at[j, r]
        )

    for j in reversed(range(blocks)):
        for r in (2, 3, 1, 0):
            x_copy(j, r).start()
    own_grad = pltpu.make_async_copy(grad_hbm, grads.at[0], own_sem)
    own_grad.start()

    barrier = pltpu.get_barrier_semaphore()

    def greet(where):
        pl.semaphore_signal(barrier, inc=1, device_id=where, device_id_type=MESH)

    for r in range(1, 4):
        greet((me, flip(rank, r)))
    for k in [1] + list(range(2, n_dp, 2)):
        greet((flip(me, k), rank))
    for j in range(1, blocks):
        greet((meet(me, turn, j), rank))

    @pl.when(turn > 0)
    def _():
        greet((meet(me, turn, 0), rank))

    own_turn = (3 - turn) // 3
    pl.semaphore_wait(barrier, 3 + n_dp // 2 + blocks - own_turn)

    def remote(src, dst, send, recv, where):
        return pltpu.make_async_remote_copy(
            src_ref=src, dst_ref=dst, send_sem=send, recv_sem=recv,
            device_id=where, device_id_type=MESH,
        )

    def grad_copy(k):
        if k % 2 == 0:
            src, where = grad_hbm, (flip(me, k), rank)
        else:
            src = grad_hbm if k == 1 else grads.at[k - 1]
            where = (flip(me, 1), rank)
        return remote(src, grads.at[k], grad_send.at[k], grad_recv.at[k], where)

    for k in reversed(range(2, n_dp, 2)):
        grad_copy(k).start()
    grad_copy(1).start()

    listed = kept_ref[...]
    place = lax.broadcasted_iota(jnp.int32, (1, keep), 1)
    slot = lax.broadcasted_iota(jnp.int32, (cap, keep), 0)
    token = lax.broadcasted_iota(jnp.int32, (tok, keep), 0)

    def one_hot(r):
        low = flip(rank, r) * tok
        start = jnp.sum(jnp.where(listed < low, 1, 0), axis=1, keepdims=True)
        inside = jnp.logical_and(listed >= low, listed < low + tok)
        target = jnp.where(inside, place - start, -1)
        return jnp.where(slot == target, 1.0, 0.0)

    hots = [one_hot(r) for r in range(4)]
    row_is = jnp.where(token == listed - rank * tok, 1.0, 0.0).astype(jnp.bfloat16)
    choose = lax.dot_general(
        hots[0].astype(jnp.bfloat16), row_is, (((1,), (1,)), ((), ())),
        preferred_element_type=jnp.float32,
    ).astype(jnp.bfloat16)

    def pre_copy(s, r):
        return remote(
            pick.at[s, r], pre.at[s, pl.ds(r * cap, cap)],
            pre_send.at[s, r], pre_recv.at[s, r], (me, flip(rank, r)),
        )

    for s, (j, h) in enumerate(steps):
        for r in (2, 3, 1, 0):
            if h == 0:
                x_copy(j, r).wait()
            part = jnp.dot(
                choose, x_buf[j, r, :, h * chunk:(h + 1) * chunk],
                preferred_element_type=jnp.float32,
            ).astype(jnp.bfloat16)
            if r:
                pick[s, r] = part
                pre_copy(s, r).start()
            else:
                pre[s, 0:cap] = part

    back = jnp.concatenate([jnp.transpose(hot) for hot in hots], axis=1).astype(jnp.bfloat16)

    def sel_copy(s, kind):
        if kind == 0:
            j = steps[s][0]
            src, to, where = comp.at[s], 0, (meet(me, turn, j), rank)
        elif kind == 3:
            src, to, where = sel.at[2, s], 3, (me, flip(rank, 1))
        else:
            src, to, where = sel.at[0, s], kind, (me, flip(rank, kind))
        return remote(src, sel.at[to, s], sel_send.at[kind, s], sel_recv.at[kind, s], where)

    def place_in_order(s):
        j = steps[s][0]
        for r in range(1, 4):
            pre_copy(s, r).wait_recv()
        rows = jnp.dot(back, pre[s], preferred_element_type=jnp.float32).astype(jnp.bfloat16)
        if j:
            comp[s] = rows
            sel_copy(s, 0).start()
        else:
            @pl.when(turn > 0)
            def _():
                comp[s] = rows
                sel_copy(s, 0).start()

            @pl.when(turn == 0)
            def _():
                sel[0, s] = rows

    def share(s):
        if steps[s][0]:
            sel_copy(s, 0).wait_recv()
        else:
            @pl.when(turn > 0)
            def _():
                sel_copy(s, 0).wait_recv()
        sel_copy(s, 2).start()
        sel_copy(s, 1).start()

    def pass_on(s):
        sel_copy(s, 2).wait_recv()
        sel_copy(s, 3).start()

    def multiply(s):
        j, h = steps[s]
        sel_copy(s, 1).wait_recv()
        sel_copy(s, 3).wait_recv()
        total = None
        for r in range(4):
            term = lax.dot_general(
                sel[r, s], grads[turns[r] + 4 * j], (((0,), (0,)), ((), ())),
                preferred_element_type=jnp.float32,
            )
            total = term if total is None else total + term
        rows = pl.ds(h * chunk, chunk)
        if j < blocks - 1:
            total = total + out_ref[rows, :]
        out_ref[rows, :] = total * scale if j == 0 else total

    count = len(steps)
    forwards = list(reversed(range(2, n_dp, 2)))
    per_step = -(-len(forwards) // max(1, min(count, 4)))
    waited = [False]

    def grads_here():
        if not waited[0]:
            own_grad.wait()
            for k in range(1, n_dp, 2):
                grad_copy(k).wait_recv()
            waited[0] = True

    for i in range(count + 4):
        if i < count:
            place_in_order(i)
        for k in forwards[:per_step]:
            grad_copy(k).wait_recv()
            grad_copy(k + 1).start()
        forwards = forwards[per_step:]
        if 0 <= i - 2 < count:
            share(i - 2)
        if 0 <= i - 3 < count:
            pass_on(i - 3)
        if 0 <= i - 4 < count:
            grads_here()
            multiply(i - 4)

    for k in range(1, n_dp):
        grad_copy(k).wait_send()
    for s, (j, h) in enumerate(steps):
        for r in range(1, 4):
            pre_copy(s, r).wait_send()
            sel_copy(s, r).wait_send()
        if j:
            sel_copy(s, 0).wait_send()
        else:
            @pl.when(turn > 0)
            def _():
                sel_copy(s, 0).wait_send()


def on_device(normed_input, grad_kv, kept):
    n_dp = lax.axis_size("dp")
    tok, width = normed_input.shape
    keep, kv = grad_kv.shape
    cols = width // n_dp
    chunk = min(CHUNK, cols)
    blocks, halves = n_dp // 4, cols // chunk
    count = blocks * halves
    scale = float(lax.axis_size("tensor") * tok) / float(keep)
    vmem, dma = pltpu.VMEM, pltpu.SemaphoreType.DMA
    bf16 = jnp.bfloat16
    return pl.pallas_call(
        functools.partial(kernel, n_dp, chunk, scale),
        out_shape=jax.ShapeDtypeStruct((cols, kv), jnp.float32),
        in_specs=[
            pl.BlockSpec(memory_space=pl.ANY),
            pl.BlockSpec(memory_space=pl.ANY),
            pl.BlockSpec(memory_space=pltpu.VMEM),
        ],
        out_specs=pl.BlockSpec(memory_space=pltpu.VMEM),
        scratch_shapes=[
            vmem((blocks, 4, tok, cols), bf16),
            vmem((count, 4, tok // 2, chunk), bf16),
            vmem((count, 2 * tok, chunk), bf16),
            vmem((count, keep, chunk), bf16),
            vmem((4, count, keep, chunk), bf16),
            vmem((n_dp, keep, kv), bf16),
            dma((blocks, 4)),
            dma,
            dma((count, 4)),
            dma((count, 4)),
            dma((4, count)),
            dma((4, count)),
            dma((n_dp,)),
            dma((n_dp,)),
        ],
        compiler_params=pltpu.CompilerParams(
            collective_id=0, has_side_effects=True, vmem_limit_bytes=48 * 1024 * 1024
        ),
        cost_estimate=pl.CostEstimate(
            flops=2 * n_dp * keep * cols * kv, bytes_accessed=8 * 1024 * 1024, transcendentals=0
        ),
    )(normed_input, grad_kv, kept)


def solution(mesh):
    return jax.shard_map(
        on_device,
        mesh=mesh,
        in_specs=(P(("dp", "tensor"), None), P("dp", "tensor"), P("dp", None)),
        out_specs=P("dp", "tensor"),
        check_vma=False,
    )
```

```python
import functools

import jax
import jax.numpy as jnp
from jax import lax
from jax.experimental import pallas as pl
from jax.experimental.pallas import tpu as pltpu
from jax.sharding import PartitionSpec as P

MESH = pl.DeviceIdType.MESH
CHUNK = 256


def flip(value, bits):
    place = 1
    result = value
    while place <= bits:
        if bits & place:
            result = result + place * (1 - 2 * ((value // place) % 2))
        place *= 2
    return result


def turn_of(rank):
    across, core = rank // 2, rank % 2
    return 2 * core + (across + core) % 2


def meet(group, turn, j):
    low = (group % 2 + turn % 2) % 2 + 2 * ((group // 2 % 2 + turn // 2) % 2)
    return low + 4 * flip(group // 4, j)


def kernel(
    n_dp, chunk, scale,
    x_hbm, grad_hbm, kept_ref, out_ref,
    x_buf, pick, pre, comp, sel, grads,
    x_sem, own_sem, pre_send, pre_recv, sel_send, sel_recv, grad_send, grad_recv,
):
    tok = x_hbm.shape[0]
    keep = kept_ref.shape[1]
    cap = tok // 2
    cols = x_hbm.shape[1] // n_dp
    halves = cols // chunk
    blocks = n_dp // 4
    me = lax.axis_index("dp")
    rank = lax.axis_index("tensor")
    turn = turn_of(rank)
    turns = [turn_of(flip(rank, r)) for r in range(4)]
    steps = [(j, h) for j in reversed(range(blocks)) for h in range(halves)]

    def x_copy(j, r):
        start = pl.multiple_of(meet(me, turns[r], j) * cols, cols)
        return pltpu.make_async_copy(
            x_hbm.at[:, pl.ds(start, cols)], x_buf.at[j, r], x_sem.at[j, r]
        )

    for j in reversed(range(blocks)):
        for r in (2, 3, 1, 0):
            x_copy(j, r).start()
    own_grad = pltpu.make_async_copy(grad_hbm, grads.at[0], own_sem)
    own_grad.start()

    barrier = pltpu.get_barrier_semaphore()
    bits = [1 << b for b in range(n_dp.bit_length() - 1)]

    def greet(where):
        pl.semaphore_signal(barrier, inc=1, device_id=where, device_id_type=MESH)

    for r in range(1, 4):
        greet((me, flip(rank, r)))
    for bit in bits:
        greet((flip(me, bit), rank))
    for j in range(1, blocks):
        greet((meet(me, turn, j), rank))

    @pl.when(turn > 0)
    def _():
        greet((meet(me, turn, 0), rank))

    listed = kept_ref[...]
    place = lax.broadcasted_iota(jnp.int32, (1, keep), 1)
    slot = lax.broadcasted_iota(jnp.int32, (cap, keep), 0)
    token = lax.broadcasted_iota(jnp.int32, (tok, keep), 0)

    def one_hot(r):
        low = flip(rank, r) * tok
        start = jnp.sum(jnp.where(listed < low, 1, 0), axis=1, keepdims=True)
        inside = jnp.logical_and(listed >= low, listed < low + tok)
        target = jnp.where(inside, place - start, -1)
        return jnp.where(slot == target, 1.0, 0.0)

    hots = [one_hot(0)]
    row_is = jnp.where(token == listed - rank * tok, 1.0, 0.0).astype(jnp.bfloat16)
    choose = lax.dot_general(
        hots[0].astype(jnp.bfloat16), row_is, (((1,), (1,)), ((), ())),
        preferred_element_type=jnp.float32,
    ).astype(jnp.bfloat16)

    own_turn = (3 - turn) // 3
    pl.semaphore_wait(barrier, 3 + len(bits) + blocks - own_turn)

    def remote(src, dst, send, recv, where):
        return pltpu.make_async_remote_copy(
            src_ref=src, dst_ref=dst, send_sem=send, recv_sem=recv,
            device_id=where, device_id_type=MESH,
        )

    def grad_copy(k):
        low = k & -k
        src = grads.at[k - low] if k > low else grad_hbm
        where = (flip(me, low), rank)
        return remote(src, grads.at[k], grad_send.at[k], grad_recv.at[k], where)

    for bit in reversed(bits):
        grad_copy(bit).start()

    def pre_copy(s, r):
        return remote(
            pick.at[s, r], pre.at[s, pl.ds(r * cap, cap)],
            pre_send.at[s, r], pre_recv.at[s, r], (me, flip(rank, r)),
        )

    for s, (j, h) in enumerate(steps):
        for r in (2, 3, 1, 0):
            if h == 0:
                x_copy(j, r).wait()
            part = jnp.dot(
                choose, x_buf[j, r, :, h * chunk:(h + 1) * chunk],
                preferred_element_type=jnp.float32,
            ).astype(jnp.bfloat16)
            if r:
                pick[s, r] = part
                pre_copy(s, r).start()
            else:
                pre[s, 0:cap] = part

    hots += [one_hot(r) for r in range(1, 4)]
    back = jnp.concatenate([jnp.transpose(hot) for hot in hots], axis=1).astype(jnp.bfloat16)

    def sel_copy(s, kind):
        if kind == 0:
            j = steps[s][0]
            src, to, where = comp.at[s], 0, (meet(me, turn, j), rank)
        elif kind == 3:
            src, to, where = sel.at[2, s], 3, (me, flip(rank, 1))
        else:
            src, to, where = sel.at[0, s], kind, (me, flip(rank, kind))
        return remote(src, sel.at[to, s], sel_send.at[kind, s], sel_recv.at[kind, s], where)

    def place_in_order(s):
        j = steps[s][0]
        for r in range(1, 4):
            pre_copy(s, r).wait_recv()
        rows = jnp.dot(back, pre[s], preferred_element_type=jnp.float32).astype(jnp.bfloat16)
        if j:
            comp[s] = rows
            sel_copy(s, 0).start()
        else:
            @pl.when(turn > 0)
            def _():
                comp[s] = rows
                sel_copy(s, 0).start()

            @pl.when(turn == 0)
            def _():
                sel[0, s] = rows

    def share(s):
        if steps[s][0]:
            sel_copy(s, 0).wait_recv()
        else:
            @pl.when(turn > 0)
            def _():
                sel_copy(s, 0).wait_recv()
        sel_copy(s, 2).start()
        sel_copy(s, 1).start()

    def pass_on(s):
        sel_copy(s, 2).wait_recv()
        sel_copy(s, 3).start()

    def multiply(s):
        j, h = steps[s]
        sel_copy(s, 1).wait_recv()
        sel_copy(s, 3).wait_recv()
        total = None
        for r in range(4):
            term = lax.dot_general(
                sel[r, s], grads[turns[r] + 4 * j], (((0,), (0,)), ((), ())),
                preferred_element_type=jnp.float32,
            )
            total = term if total is None else total + term
        rows = pl.ds(h * chunk, chunk)
        if j < blocks - 1:
            total = total + out_ref[rows, :]
        out_ref[rows, :] = total * scale if j == 0 else total

    count = len(steps)
    forwards = list(range(2, n_dp, 2))
    moments = [2, 3, 5]
    per_moment = -(-len(forwards) // len(moments))
    grads_ready = set()

    def grads_here(j):
        if j in grads_ready:
            return
        grads_ready.add(j)
        if j == 0:
            own_grad.wait()
        for k in (4 * j + 1, 4 * j + 3):
            grad_copy(k).wait_recv()

    done = 0
    for i in range(max(count, 6) + 4):
        if i < count:
            place_in_order(i)
        if i in moments:
            for k in forwards[:per_moment]:
                grad_copy(k).wait_recv()
                low = (k & -k) // 2
                while low:
                    grad_copy(k + low).start()
                    low //= 2
            forwards = forwards[per_moment:]
        if 0 <= i - 2 < count:
            share(i - 2)
        if 0 <= i - 3 < count:
            pass_on(i - 3)
        if i >= 7:
            for _ in range(2):
                if done < count and done <= i - 4:
                    grads_here(steps[done][0])
                    multiply(done)
                    done += 1
    while done < count:
        grads_here(steps[done][0])
        multiply(done)
        done += 1

    for k in range(1, n_dp):
        grad_copy(k).wait_send()
    for s, (j, h) in enumerate(steps):
        for r in range(1, 4):
            pre_copy(s, r).wait_send()
            sel_copy(s, r).wait_send()
        if j:
            sel_copy(s, 0).wait_send()
        else:
            @pl.when(turn > 0)
            def _():
                sel_copy(s, 0).wait_send()


def on_device(normed_input, grad_kv, kept):
    n_dp = lax.axis_size("dp")
    tok, width = normed_input.shape
    keep, kv = grad_kv.shape
    cols = width // n_dp
    chunk = min(CHUNK, cols)
    blocks, halves = n_dp // 4, cols // chunk
    count = blocks * halves
    scale = float(lax.axis_size("tensor") * tok) / float(keep)
    vmem, dma = pltpu.VMEM, pltpu.SemaphoreType.DMA
    bf16 = jnp.bfloat16
    return pl.pallas_call(
        functools.partial(kernel, n_dp, chunk, scale),
        out_shape=jax.ShapeDtypeStruct((cols, kv), jnp.float32),
        in_specs=[
            pl.BlockSpec(memory_space=pl.ANY),
            pl.BlockSpec(memory_space=pl.ANY),
            pl.BlockSpec(memory_space=pltpu.VMEM),
        ],
        out_specs=pl.BlockSpec(memory_space=pltpu.VMEM),
        scratch_shapes=[
            vmem((blocks, 4, tok, cols), bf16),
            vmem((count, 4, tok // 2, chunk), bf16),
            vmem((count, 2 * tok, chunk), bf16),
            vmem((count, keep, chunk), bf16),
            vmem((4, count, keep, chunk), bf16),
            vmem((n_dp, keep, kv), bf16),
            dma((blocks, 4)),
            dma,
            dma((count, 4)),
            dma((count, 4)),
            dma((4, count)),
            dma((4, count)),
            dma((n_dp,)),
            dma((n_dp,)),
        ],
        compiler_params=pltpu.CompilerParams(
            collective_id=0, has_side_effects=True, vmem_limit_bytes=60 * 1024 * 1024
        ),
        cost_estimate=pl.CostEstimate(
            flops=2 * n_dp * keep * cols * kv, bytes_accessed=8 * 1024 * 1024, transcendentals=0
        ),
    )(normed_input, grad_kv, kept)


def solution(mesh):
    return jax.shard_map(
        on_device,
        mesh=mesh,
        in_specs=(P(("dp", "tensor"), None), P("dp", "tensor"), P("dp", None)),
        out_specs=P("dp", "tensor"),
        check_vma=False,
    )
```

```python
import functools

import jax
import jax.numpy as jnp
from jax import lax
from jax.experimental import pallas as pl
from jax.experimental.pallas import tpu as pltpu
from jax.sharding import PartitionSpec as P

MESH = pl.DeviceIdType.MESH
CHUNK = 256


def flip(value, bits):
    place = 1
    result = value
    while place <= bits:
        if bits & place:
            result = result + place * (1 - 2 * ((value // place) % 2))
        place *= 2
    return result


def turn_of(rank):
    across, core = rank // 2, rank % 2
    return 2 * core + (across + core) % 2


def meet(group, turn, j):
    low = (group % 2 + turn % 2) % 2 + 2 * ((group // 2 % 2 + turn // 2) % 2)
    return low + 4 * flip(group // 4, j)


def kernel(
    n_dp, chunk, scale,
    x_hbm, grad_hbm, kept_ref, out_ref,
    x_buf, pick, pre, comp, sel, grads,
    x_sem, own_sem, pre_send, pre_recv, sel_send, sel_recv, grad_send, grad_recv,
):
    tok = x_hbm.shape[0]
    keep = kept_ref.shape[1]
    cap = tok // 2
    cols = x_hbm.shape[1] // n_dp
    halves = cols // chunk
    blocks = n_dp // 4
    me = lax.axis_index("dp")
    rank = lax.axis_index("tensor")
    turn = turn_of(rank)
    turns = [turn_of(flip(rank, r)) for r in range(4)]
    steps = [(j, h) for j in reversed(range(blocks)) for h in range(halves)]

    def x_copy(j, r):
        start = pl.multiple_of(meet(me, turns[r], j) * cols, cols)
        return pltpu.make_async_copy(
            x_hbm.at[:, pl.ds(start, cols)], x_buf.at[j, r], x_sem.at[j, r]
        )

    for j in reversed(range(blocks)):
        for r in (2, 3, 1, 0):
            x_copy(j, r).start()
    own_grad = pltpu.make_async_copy(grad_hbm, grads.at[0], own_sem)
    own_grad.start()

    barrier = pltpu.get_barrier_semaphore()
    bits = [1 << b for b in range(n_dp.bit_length() - 1)]

    def greet(where):
        pl.semaphore_signal(barrier, inc=1, device_id=where, device_id_type=MESH)

    for r in range(1, 4):
        greet((me, flip(rank, r)))
    for bit in bits:
        greet((flip(me, bit), rank))
    for j in range(1, blocks):
        greet((meet(me, turn, j), rank))

    @pl.when(turn > 0)
    def _():
        greet((meet(me, turn, 0), rank))

    listed = kept_ref[...]
    place = lax.broadcasted_iota(jnp.int32, (1, keep), 1)
    slot = lax.broadcasted_iota(jnp.int32, (cap, keep), 0)
    token = lax.broadcasted_iota(jnp.int32, (tok, keep), 0)

    def one_hot(r):
        low = flip(rank, r) * tok
        start = jnp.sum(jnp.where(listed < low, 1, 0), axis=1, keepdims=True)
        inside = jnp.logical_and(listed >= low, listed < low + tok)
        target = jnp.where(inside, place - start, -1)
        return jnp.where(slot == target, 1.0, 0.0)

    hots = [one_hot(0)]
    row_is = jnp.where(token == listed - rank * tok, 1.0, 0.0).astype(jnp.bfloat16)
    choose = lax.dot_general(
        hots[0].astype(jnp.bfloat16), row_is, (((1,), (1,)), ((), ())),
        preferred_element_type=jnp.float32,
    ).astype(jnp.bfloat16)

    own_turn = (3 - turn) // 3
    pl.semaphore_wait(barrier, 3 + len(bits) + blocks - own_turn)

    def remote(src, dst, send, recv, where):
        return pltpu.make_async_remote_copy(
            src_ref=src, dst_ref=dst, send_sem=send, recv_sem=recv,
            device_id=where, device_id_type=MESH,
        )

    def grad_copy(k):
        low = k & -k
        src = grads.at[k - low] if k > low else grad_hbm
        where = (flip(me, low), rank)
        return remote(src, grads.at[k], grad_send.at[k], grad_recv.at[k], where)

    for bit in reversed(bits):
        grad_copy(bit).start()

    def pre_copy(s, r):
        return remote(
            pick.at[s, r], pre.at[s, pl.ds(r * cap, cap)],
            pre_send.at[s, r], pre_recv.at[s, r], (me, flip(rank, r)),
        )

    for s, (j, h) in enumerate(steps):
        for r in (2, 3, 1, 0):
            if h == 0:
                x_copy(j, r).wait()
            part = jnp.dot(
                choose, x_buf[j, r, :, h * chunk:(h + 1) * chunk],
                preferred_element_type=jnp.float32,
            ).astype(jnp.bfloat16)
            if r:
                pick[s, r] = part
                pre_copy(s, r).start()
            else:
                pre[s, 0:cap] = part

    hots += [one_hot(r) for r in range(1, 4)]
    back = jnp.concatenate([jnp.transpose(hot) for hot in hots], axis=1).astype(jnp.bfloat16)

    def sel_copy(s, kind):
        if kind == 0:
            j = steps[s][0]
            src, to, where = comp.at[s], 0, (meet(me, turn, j), rank)
        elif kind == 3:
            src, to, where = sel.at[2, s], 3, (me, flip(rank, 1))
        else:
            src, to, where = sel.at[0, s], kind, (me, flip(rank, kind))
        return remote(src, sel.at[to, s], sel_send.at[kind, s], sel_recv.at[kind, s], where)

    def place_in_order(s):
        j = steps[s][0]
        for r in range(1, 4):
            pre_copy(s, r).wait_recv()
        rows = jnp.dot(back, pre[s], preferred_element_type=jnp.float32).astype(jnp.bfloat16)
        if j:
            comp[s] = rows
            sel_copy(s, 0).start()
        else:
            @pl.when(turn > 0)
            def _():
                comp[s] = rows
                sel_copy(s, 0).start()

            @pl.when(turn == 0)
            def _():
                sel[0, s] = rows

    def share(s):
        if steps[s][0]:
            sel_copy(s, 0).wait_recv()
        else:
            @pl.when(turn > 0)
            def _():
                sel_copy(s, 0).wait_recv()
        sel_copy(s, 2).start()
        sel_copy(s, 1).start()

    def pass_on(s):
        sel_copy(s, 2).wait_recv()
        sel_copy(s, 3).start()

    def multiply(s):
        j, h = steps[s]
        sel_copy(s, 1).wait_recv()
        sel_copy(s, 3).wait_recv()
        total = None
        for r in range(4):
            term = lax.dot_general(
                sel[r, s], grads[turns[r] + 4 * j], (((0,), (0,)), ((), ())),
                preferred_element_type=jnp.float32,
            )
            total = term if total is None else total + term
        rows = pl.ds(h * chunk, chunk)
        if j < blocks - 1:
            total = total + out_ref[rows, :]
        out_ref[rows, :] = total * scale if j == 0 else total

    count = len(steps)
    forwards = list(range(2, n_dp, 2))
    moments = [2, 3, 5]
    per_moment = -(-len(forwards) // len(moments))
    grads_ready = set()

    def grads_here(j):
        if j in grads_ready:
            return
        grads_ready.add(j)
        if j == 0:
            own_grad.wait()
        for k in (4 * j + 1, 4 * j + 3):
            grad_copy(k).wait_recv()

    done = 0
    for i in range(max(count, 6) + 4):
        if i < count:
            place_in_order(i)
        if i in moments:
            for k in forwards[:per_moment]:
                grad_copy(k).wait_recv()
                low = (k & -k) // 2
                while low:
                    grad_copy(k + low).start()
                    low //= 2
            forwards = forwards[per_moment:]
        if 0 <= i - 2 < count:
            share(i - 2)
        if 0 <= i - 3 < count:
            pass_on(i - 3)
        if i >= 7:
            for _ in range(2):
                if done < count and done <= i - 4:
                    grads_here(steps[done][0])
                    multiply(done)
                    done += 1
    while done < count:
        grads_here(steps[done][0])
        multiply(done)
        done += 1

    for k in range(1, n_dp):
        grad_copy(k).wait_send()
    for s, (j, h) in enumerate(steps):
        for r in range(1, 4):
            pre_copy(s, r).wait_send()
            sel_copy(s, r).wait_send()
        if j:
            sel_copy(s, 0).wait_send()
        else:
            @pl.when(turn > 0)
            def _():
                sel_copy(s, 0).wait_send()


def on_device(normed_input, grad_kv, kept):
    n_dp = lax.axis_size("dp")
    tok, width = normed_input.shape
    keep, kv = grad_kv.shape
    cols = width // n_dp
    chunk = min(CHUNK, cols)
    blocks, halves = n_dp // 4, cols // chunk
    count = blocks * halves
    scale = float(lax.axis_size("tensor") * tok) / float(keep)
    vmem, dma = pltpu.VMEM, pltpu.SemaphoreType.DMA
    bf16 = jnp.bfloat16
    return pl.pallas_call(
        functools.partial(kernel, n_dp, chunk, scale),
        out_shape=jax.ShapeDtypeStruct((cols, kv), jnp.float32),
        in_specs=[
            pl.BlockSpec(memory_space=pl.ANY),
            pl.BlockSpec(memory_space=pl.ANY),
            pl.BlockSpec(memory_space=pltpu.VMEM),
        ],
        out_specs=pl.BlockSpec(memory_space=pltpu.VMEM),
        scratch_shapes=[
            vmem((blocks, 4, tok, cols), bf16),
            vmem((count, 4, tok // 2, chunk), bf16),
            vmem((count, 2 * tok, chunk), bf16),
            vmem((count, keep, chunk), bf16),
            vmem((4, count, keep, chunk), bf16),
            vmem((n_dp, keep, kv), bf16),
            dma((blocks, 4)),
            dma,
            dma((count, 4)),
            dma((count, 4)),
            dma((4, count)),
            dma((4, count)),
            dma((n_dp,)),
            dma((n_dp,)),
        ],
        compiler_params=pltpu.CompilerParams(
            collective_id=0, has_side_effects=True, vmem_limit_bytes=48 * 1024 * 1024
        ),
        cost_estimate=pl.CostEstimate(
            flops=2 * n_dp * keep * cols * kv, bytes_accessed=8 * 1024 * 1024, transcendentals=0
        ),
    )(normed_input, grad_kv, kept)


def solution(mesh):
    return jax.shard_map(
        on_device,
        mesh=mesh,
        in_specs=(P(("dp", "tensor"), None), P("dp", "tensor"), P("dp", None)),
        out_specs=P("dp", "tensor"),
        check_vma=False,
    )
```
